32 devices in a mesh: rep: 2 (over y), pipe: 8 (over z, x), tp: 2 (over core).
Axes of the slice: x: 2, y: 2, z: 4, core: 2. Of those that a mesh axis runs over, the one named last changes fastest.
Arguments:
- act_forward: bfloat16 [8, 2, 128, 4096], P('pipe', 'rep', 'tp'), may hold values from -6 to 6
- act_saved: bfloat16 [8, 2, 128, 4096], P('pipe', 'rep', 'tp'), may hold values from -6 to 6
- grad_output: bfloat16 [8, 2, 128, 4096], P('pipe', 'rep', 'tp'), may hold values from -6 to 6
- norm_gain: bfloat16 [8, 4096], P('pipe'), may hold values from 0.099609375 to 1.8984375
- up_weight: bfloat16 [8, 4096, 14336], P('pipe', None, ('rep', 'tp')), may hold values from -0.09375 to 0.09375
- down_weight: bfloat16 [8, 14336, 4096], P('pipe', ('rep', 'tp')), may hold values from -0.046875 to 0.046875
- section_layers: int32 [4], replicated, may hold values from 1 to 3, 8 in all
- redirect_count: int32 [3, 2], replicated, may hold values from 0 to 3, as said below
- redirect_dest: int32 [3, 2], replicated, may hold values from 0 to 1, as said below
Outputs:
- arrive_forward: bfloat16 [8, 2, 128, 4096], P('pipe', 'rep', 'tp')
- arrive_backward: bfloat16 [8, 2, 128, 4096], P('pipe', 'rep', 'tp')
The draws below stay inside these ranges and needn't reach their ends.
Inputs may be any that keep to these rules, and one draw needn't show every extreme that they name: `redirect_count`: counts are in blocks of 16 rows. At each boundary every replica either sends to another replica or has count zero; a sender's destination has count zero there, and each replica receives from at most one sender. Following the boundaries in order from 5 live blocks, every replica keeps at least one block and never holds more than 8. At the first boundary every sender sends to the replica 2 / 2 indices away (counted round); one replica sends exactly 3 blocks, filling its receiver to 8, and with four or more replicas another replica sends exactly one block. `redirect_dest`: the destination of a replica with count zero is the replica itself.
All inputs are finite; a program needn't handle non-finite values.
Results may differ from the reference program's by a relative error of at most 0.015.
Values may be sent and summed in bfloat16 or wider, within the bound.
A program may use at most 128 MiB of HBM per device.

```python
import math
import jax
import jax.numpy as jnp
import numpy as np
from jax import lax

D = 4096
FF = 14336
CAP = 128
BLOCK = 16
MOST_LAYERS = 3
SECTIONS = 4
CAPB = 8
MOST = 3
START = 5
N_REP = 2
N_PIPE = 8
N_TP = 2


def redirect_plan(key):
    base_key = jax.random.fold_in(key, 4049)
    live_blocks = jnp.full((N_REP,), START, jnp.int32)
    count_rows = []
    dest_rows = []
    half_reps = N_REP // 2
    first_start = jax.random.randint(jax.random.fold_in(base_key, 7001), (), 0, N_REP, dtype=jnp.int32)
    lanes = jnp.arange(half_reps, dtype=jnp.int32)
    first_order = jnp.stack([(first_start + lanes) % N_REP, (first_start + lanes + half_reps) % N_REP], axis=1).reshape(N_REP).astype(jnp.int32)
    swapped_index = jnp.arange(N_REP, dtype=jnp.int32) ^ 1
    for boundary in range(SECTIONS - 1):
        step_key = jax.random.fold_in(base_key, boundary)
        if boundary == 0:
            shuffled = first_order
        elif boundary == 1:
            shuffled = jnp.take(first_order, swapped_index)
        else:
            shuffled = jax.random.permutation(jax.random.fold_in(step_key, 0), N_REP).astype(jnp.int32)
        count_row = jnp.zeros((N_REP,), jnp.int32)
        dest_row = jnp.arange(N_REP, dtype=jnp.int32)
        for pair_index in range(N_REP // 2):
            sender = shuffled[2 * pair_index]
            receiver = shuffled[2 * pair_index + 1]
            ceiling = jnp.minimum(jnp.minimum(live_blocks[sender] - 1, CAPB - live_blocks[receiver]), MOST).astype(jnp.int32)
            pair_key = jax.random.fold_in(step_key, pair_index + 1)
            if boundary == 0 and pair_index == 0:
                amount = ceiling
            elif boundary == 0 and pair_index == 1:
                amount = jnp.minimum(ceiling, 1).astype(jnp.int32)
            elif boundary == 1 and pair_index == 0:
                amount = jax.random.randint(pair_key, (), 1, jnp.maximum(ceiling, 1) + 1, dtype=jnp.int32)
                amount = jnp.minimum(amount, ceiling).astype(jnp.int32)
            else:
                amount = jax.random.randint(pair_key, (), 0, ceiling + 1, dtype=jnp.int32)
            count_row = count_row.at[sender].set(amount)
            dest_row = dest_row.at[sender].set(jnp.where(amount > 0, receiver, sender).astype(jnp.int32))
            live_blocks = live_blocks.at[sender].add(-amount).at[receiver].add(amount)
        count_rows.append(count_row)
        dest_rows.append(dest_row)
    return (jnp.stack(count_rows), jnp.stack(dest_rows))


def draw_redirect_count(key, part):
    return redirect_plan(key)[0]


def draw_redirect_dest(key, part):
    return redirect_plan(key)[1]


def block_scale(stream_key, dims, pieces, low, largest):
    loudness, own = 1.0, jax.random.fold_in(stream_key, 6)
    for axis_at, parts in pieces:
        steps = jnp.exp(jax.random.uniform(jax.random.fold_in(own, axis_at), (parts,), jnp.float32, low / len(pieces), largest / len(pieces)))
        loudness = loudness * jnp.repeat(steps, dims[axis_at] // parts).reshape([-1 if axis == axis_at else 1 for axis in range(len(dims))])
    return loudness


def length_profile(count, total, bound, skew):
    portions = [(1 << 20) // math.isqrt(grade ** skew) + 1 for grade in range(2, count + 1)]
    surplus, given = total - bound - (count - 1), [1] * (count - 1)
    while surplus > 0:
        candidates = [i for i in range(count - 1) if given[i] < bound]
        whole, left = sum([portions[i] for i in candidates]), surplus
        for i in candidates:
            extra = min(bound - given[i], max(1, left * portions[i] // whole), surplus)
            given[i] = given[i] + extra
            surplus = surplus - extra
    return np.array([bound] + given)


def ragged(key, count, total, bound, skew):
    if count == 2:
        one = jax.random.randint(key, (), max(1, total - bound), min(bound, total - 1) + 1)
        return jnp.stack([one, total - one])
    sizes = jnp.asarray(length_profile(count, total, bound, skew), jnp.int32)
    pairs = (count - 1) // 2
    giver, taker = sizes[1:1 + 2 * pairs:2], sizes[2:2 + 2 * pairs:2]
    margin = jnp.minimum(giver - 1, bound - taker)
    moved = jax.random.randint(jax.random.fold_in(key, 1), (pairs,), 0, 1 << 20) % (margin + 1)
    sizes = sizes.at[1:1 + 2 * pairs:2].set(giver - moved).at[2:2 + 2 * pairs:2].set(taker + moved)
    return sizes[jax.random.permutation(jax.random.fold_in(key, 2), count)]


def noise(own_key, dims, scale, reach, pieces=(), kind=jnp.bfloat16):
    values = jax.random.normal(own_key, dims, jnp.float32) * scale
    if len(pieces) > 0:
        values = block_scale(own_key, dims, pieces, -0.22, 0.18) * values
    return jnp.clip(values, min=-reach, max=reach).astype(kind)


def setup_inputs(seed: int = 0) -> dict:
    key_list = jax.random.split(jax.random.key(seed), 10)
    return {
        "act_forward": noise(key_list[0], (N_PIPE, N_REP, CAP, D), 1.0, 6.0, ((0, 8), (1, 2), (2, 2))),
        "act_saved": noise(key_list[1], (N_PIPE, N_REP, CAP, D), 1.0, 6.0, ((0, 8), (1, 2), (2, 2))),
        "grad_output": noise(key_list[2], (N_PIPE, N_REP, CAP, D), 1.0, 6.0, ((0, 8), (1, 2), (2, 2))),
        "norm_gain": jnp.clip(1.0 + 0.18 * jax.random.normal(key_list[3], (N_PIPE, D), jnp.float32), 0.099609375, 1.8984375).astype(jnp.bfloat16),
        "up_weight": noise(key_list[4], (N_PIPE, D, FF), D ** -0.5, 0.09375, ((0, 8), (2, 4))),
        "down_weight": noise(key_list[5], (N_PIPE, FF, D), FF ** -0.5, 0.046875, ((0, 8), (1, 4))),
        "section_layers": ragged(key_list[6], SECTIONS, N_PIPE, MOST_LAYERS, 0).astype(jnp.int32),
        "redirect_count": draw_redirect_count(jax.random.fold_in(key_list[9], 71), 0),
        "redirect_dest": draw_redirect_dest(jax.random.fold_in(key_list[9], 71), 0),
    }


EPSILON = 1e-05

def moved_blocks(counts, dests, replica_ids):
    return jnp.where((dests != replica_ids) & (counts > 0), counts, 0).astype(jnp.int32)

def section_plan(section_layers, redirect_count, redirect_dest, segments, replicas):
    replica_ids = jnp.arange(replicas, dtype=jnp.int32)
    section_ends = (jnp.cumsum(section_layers).astype(jnp.int32) - 1)[:-1]
    positions = jnp.arange(segments, dtype=jnp.int32)
    matches = (section_ends[None, :] == positions[:, None]).astype(jnp.int32)
    segment_count = lax.optimization_barrier(jnp.sum(matches[:, :, None] * redirect_count[None, :, :], axis=1)).astype(jnp.int32)
    has_boundary = lax.optimization_barrier(jnp.sum(matches, axis=1)).astype(jnp.int32)[:, None]
    segment_dest = (lax.optimization_barrier(jnp.sum(matches[:, :, None] * redirect_dest[None, :, :], axis=1)).astype(jnp.int32) + (1 - has_boundary) * replica_ids[None, :]).astype(jnp.int32)
    live_list = [jnp.full((replicas,), START, jnp.int32)]
    for position in range(segments - 1):
        moved = moved_blocks(segment_count[position], segment_dest[position], replica_ids)
        incoming = lax.optimization_barrier(jnp.sum(jnp.where(segment_dest[position][:, None] == replica_ids[None, :], moved[:, None], 0), axis=0)).astype(jnp.int32)
        live_list.append((live_list[-1] - moved + incoming).astype(jnp.int32))
    return (jnp.stack(live_list), segment_count, segment_dest)

def source_rows(live_before, counts, dests, replicas):
    replica_ids = jnp.arange(replicas, dtype=jnp.int32)
    block_ids = jnp.arange(CAPB, dtype=jnp.int32)
    moved = moved_blocks(counts, dests, replica_ids)
    sends = moved > 0
    same_dest = (dests[None, :] == dests[:, None]) & (replica_ids[None, :] < replica_ids[:, None]) & sends[None, :]
    kept = (live_before - moved).astype(jnp.int32)
    incoming = lax.optimization_barrier(jnp.sum(jnp.where(sends[:, None] & (dests[:, None] == replica_ids[None, :]), moved[:, None], 0), axis=0)).astype(jnp.int32)
    offset = lax.optimization_barrier(jnp.sum(jnp.where(same_dest, moved[None, :], 0), axis=1)).astype(jnp.int32)
    hits = sends[None, None, :] & (dests[None, None, :] == replica_ids[:, None, None]) & (block_ids[None, :, None] >= offset[None, None, :]) & (block_ids[None, :, None] < (offset + moved)[None, None, :])
    from_block = replica_ids[None, None, :] * CAPB + block_ids[None, :, None] - offset[None, None, :]
    moved_source = lax.optimization_barrier(jnp.sum(jnp.where(hits, from_block, 0), axis=2)).astype(jnp.int32)
    own_local = block_ids[None, :] - incoming[:, None]
    own_ok = (own_local >= 0) & (own_local < kept[:, None])
    own_block = own_local + moved[:, None]
    source_block = jnp.where(jnp.any(hits, axis=2), moved_source, jnp.where(own_ok, replica_ids[:, None] * CAPB + own_block, -1)).astype(jnp.int32)
    row_ids = source_block[:, :, None] * BLOCK + jnp.arange(BLOCK, dtype=jnp.int32)[None, None, :]
    return jnp.where(source_block[:, :, None] >= 0, row_ids, -1).reshape(replicas * CAPB * BLOCK).astype(jnp.int32)

def inverse_rows(source):
    total = source.shape[0]
    target = jnp.where(source >= 0, source, total).astype(jnp.int32)
    return jnp.full((total,), -1, jnp.int32).at[target].set(jnp.arange(total, dtype=jnp.int32), mode='drop')

def pick_rows(values, index):
    taken = jnp.take(values, jnp.maximum(index, 0), axis=0)
    return jnp.where(index[:, None] >= 0, taken, jnp.zeros((), values.dtype))

def normalize(values, gain_row):
    wide = values.astype(jnp.float32)
    scale = lax.rsqrt(lax.optimization_barrier(jnp.mean(wide * wide, axis=-1, keepdims=True)) + EPSILON)
    return (wide * scale * gain_row.astype(jnp.float32)).astype(jnp.bfloat16)

def norm_back(values, gain_row, upstream):
    wide = values.astype(jnp.float32)
    scale = lax.rsqrt(lax.optimization_barrier(jnp.mean(wide * wide, axis=-1, keepdims=True)) + EPSILON)
    weighted = gain_row.astype(jnp.float32) * upstream
    return scale * weighted - wide * (scale * scale * scale) * lax.optimization_barrier(jnp.mean(weighted * wide, axis=-1, keepdims=True))

def silu_slope(upper):
    sigma = jax.nn.sigmoid(upper)
    return sigma * (1.0 + upper * (1.0 - sigma))

def grouped_product(left, right, groups):
    group_width = left.shape[1] // groups

    def add_group(total, group_index):
        first_col = group_index * group_width
        piece = jnp.dot(lax.dynamic_slice_in_dim(left, first_col, group_width, 1), lax.dynamic_slice_in_dim(right, first_col, group_width, 0), preferred_element_type=jnp.float32)
        rounded = lax.optimization_barrier(piece.astype(jnp.bfloat16))
        return (total + rounded.astype(jnp.float32), None)
    total, unused = lax.scan(add_group, jnp.zeros((left.shape[0], right.shape[1]), jnp.float32), jnp.arange(groups, dtype=jnp.int32))
    return total

def reference(act_forward, act_saved, grad_output, norm_gain, up_weight, down_weight, section_layers, redirect_count, redirect_dest):
    segments = N_PIPE
    replicas = N_REP
    groups = N_REP * N_TP
    total_rows = replicas * CAP
    live, segment_count, segment_dest = section_plan(section_layers, redirect_count, redirect_dest, segments, replicas)
    empty = jnp.zeros((replicas, CAP, D), jnp.bfloat16)
    arrive_forward = [empty]
    arrive_backward = []
    for segment_index in range(segments):
        gain_row = norm_gain[segment_index]
        if segment_index < segments - 1:
            fresh = act_forward[segment_index].reshape(total_rows, D)
            hidden = jax.nn.silu(jnp.dot(normalize(fresh, gain_row), up_weight[segment_index], preferred_element_type=jnp.float32)).astype(jnp.bfloat16)
            mixed = grouped_product(hidden, down_weight[segment_index], groups)
            result = (fresh.astype(jnp.float32) + mixed).astype(jnp.bfloat16)
            later = source_rows(live[segment_index], segment_count[segment_index], segment_dest[segment_index], replicas)
            arrive_forward.append(pick_rows(result, later).reshape(replicas, CAP, D))
        if segment_index > 0:
            saved = act_saved[segment_index].reshape(total_rows, D)
            upstream = grad_output[segment_index].reshape(total_rows, D)
            upper = jnp.dot(normalize(saved, gain_row), up_weight[segment_index], preferred_element_type=jnp.float32)
            back_hidden = (jnp.dot(upstream, down_weight[segment_index].T, preferred_element_type=jnp.float32) * silu_slope(upper)).astype(jnp.bfloat16)
            returned = grouped_product(back_hidden, up_weight[segment_index].T, groups)
            gradient = (upstream.astype(jnp.float32) + norm_back(saved, gain_row, returned)).astype(jnp.bfloat16)
            earlier = inverse_rows(source_rows(live[segment_index - 1], segment_count[segment_index - 1], segment_dest[segment_index - 1], replicas))
            arrive_backward.append(pick_rows(gradient, earlier).reshape(replicas, CAP, D))
    arrive_backward.append(empty)
    return (jnp.stack(arrive_forward), jnp.stack(arrive_backward))
```

```python
import functools

import jax
import jax.numpy as jnp
from jax import lax
from jax.experimental import pallas as pl
from jax.experimental.pallas import tpu as pltpu
from jax.sharding import PartitionSpec as P

BLOCK = 16
CAPB = 8
START = 5
EPSILON = 1e-05
VMEM_LIMIT = 52 * 1024 * 1024


def from_behind(block, axis, distance):
    devices = range(lax.axis_size(axis))
    route = [(i - distance, i) for i in devices if i - distance in devices]
    return lax.ppermute(block, axis, route)


def plan_kernel(replicas, per_shard, where_ref, layers_ref, count_ref, dest_ref, out_ref):
    bounds = layers_ref.shape[0] - 1
    position = where_ref[0]
    zero = jnp.int32(0)
    ends, seen = [], jnp.int32(-1)
    for s in range(bounds):
        seen = seen + layers_ref[s]
        ends.append(seen)
    moved = [
        [
            jnp.where((dest_ref[s, r] != r) & (count_ref[s, r] > 0), count_ref[s, r], 0)
            for r in range(replicas)
        ]
        for s in range(bounds)
    ]

    def place(replica, block):
        return (lax.div(block, per_shard) * replicas + replica) * per_shard + lax.rem(block, per_shard)

    for which in range(2):
        at = position if which == 0 else jnp.maximum(position - 1, 0)
        live = [jnp.int32(START) for _ in range(replicas)]
        mine = [zero for _ in range(replicas)]
        to = [jnp.int32(r) for r in range(replicas)]
        for s in range(bounds):
            before, here = ends[s] < at, ends[s] == at
            for q in range(replicas):
                gain = -moved[s][q]
                for r in range(replicas):
                    gain = gain + jnp.where(dest_ref[s, r] == q, moved[s][r], 0)
                live[q] = live[q] + jnp.where(before, gain, 0)
                mine[q] = jnp.where(here, moved[s][q], mine[q])
                to[q] = jnp.where(here, dest_ref[s, q], to[q])
        incoming = [
            sum((jnp.where(to[r] == q, mine[r], 0) for r in range(replicas)), zero)
            for q in range(replicas)
        ]
        offset = [
            sum((jnp.where(to[o] == to[r], mine[o], 0) for o in range(r)), zero)
            for r in range(replicas)
        ]
        filled = zero
        for q in range(replicas):
            for k in range(CAPB):
                local = k - incoming[q]
                own = (local >= 0) & (local < live[q] - mine[q])
                source = jnp.where(own, place(jnp.int32(q), jnp.maximum(local + mine[q], 0)), -1)
                for r in range(replicas):
                    hit = (mine[r] > 0) & (to[r] == q) & (k >= offset[r]) & (k < offset[r] + mine[r])
                    source = jnp.where(
                        hit, place(jnp.int32(r), jnp.maximum(k - offset[r], 0)), source
                    )
                target = place(jnp.int32(q), jnp.int32(k))
                out_ref[2 * which, filled] = jnp.maximum(source, 0)
                out_ref[2 * which + 1, filled] = target
                filled = filled + jnp.where(source >= 0, 1, 0)


def make_plan(where, section_layers, redirect_count, redirect_dest, replicas, per_shard):
    return pl.pallas_call(
        functools.partial(plan_kernel, replicas, per_shard),
        out_shape=jax.ShapeDtypeStruct((4, replicas * CAPB + 1), jnp.int32),
        in_specs=[pl.BlockSpec(memory_space=pltpu.SMEM)] * 4,
        out_specs=pl.BlockSpec(memory_space=pltpu.SMEM),
    )(where, section_layers, redirect_count, redirect_dest)


def normalize(values, gain_row):
    wide = values.astype(jnp.float32)
    scale = lax.rsqrt(jnp.mean(wide * wide, axis=-1, keepdims=True) + EPSILON)
    return (wide * scale * gain_row.astype(jnp.float32)).astype(jnp.bfloat16)


def norm_back(values, gain_row, upstream):
    wide = values.astype(jnp.float32)
    scale = lax.rsqrt(jnp.mean(wide * wide, axis=-1, keepdims=True) + EPSILON)
    weighted = gain_row.astype(jnp.float32) * upstream
    return scale * weighted - wide * (scale * scale * scale) * jnp.mean(
        weighted * wide, axis=-1, keepdims=True
    )


def silu_slope(upper):
    sigma = jax.nn.sigmoid(upper)
    return sigma * (1.0 + upper * (1.0 - sigma))


def dot(left, right, contract):
    return lax.dot_general(
        left, right, ((contract[:1], contract[1:]), ((), ())), preferred_element_type=jnp.float32
    )


def rows_of(block):
    return pl.ds(pl.multiple_of(block * BLOCK, BLOCK), BLOCK)


def forward_kernel(
    blocks, per_shard, plan_ref, where_ref, fresh_ref, gain_ref, up_ref, down_ref,
    sum_ref, mine_ref, normed, total,
):
    step = pl.program_id(0)

    @pl.when(step == 0)
    def _():
        total[...] = jnp.zeros_like(total)
        mine_ref[...] = jnp.zeros_like(mine_ref)

        @pl.loop(0, blocks)
        def _(b):
            values = fresh_ref[rows_of(plan_ref[0, b]), :]
            normed[rows_of(b), :] = normalize(values, gain_ref[...])
            local = plan_ref[1, b] - where_ref[1] * per_shard

            @pl.when((local >= 0) & (local < per_shard))
            def _():
                mine_ref[rows_of(local), :] = values

    hidden = jax.nn.silu(dot(normed[...], up_ref[...], (1, 0))).astype(jnp.bfloat16)
    total[...] += dot(hidden, down_ref[...], (1, 0))

    @pl.when(step == pl.num_programs(0) - 1)
    def _():
        sum_ref[...] = jnp.zeros_like(sum_ref)

        @pl.loop(0, blocks)
        def _(b):
            sum_ref[rows_of(plan_ref[1, b]), :] = total[rows_of(b), :].astype(jnp.bfloat16)


def backward_kernel(
    blocks, per_shard, plan_ref, where_ref, saved_ref, grad_ref, gain_ref, up_ref, down_ref,
    sum_ref, mine_saved_ref, mine_grad_ref, normed, upstream, total,
):
    step = pl.program_id(0)

    @pl.when(step == 0)
    def _():
        total[...] = jnp.zeros_like(total)
        mine_saved_ref[...] = jnp.zeros_like(mine_saved_ref)
        mine_grad_ref[...] = jnp.zeros_like(mine_grad_ref)

        @pl.loop(0, blocks)
        def _(b):
            source = rows_of(plan_ref[3, b])
            values = saved_ref[source, :]
            grads = grad_ref[source, :]
            normed[rows_of(b), :] = normalize(values, gain_ref[...])
            upstream[rows_of(b), :] = grads
            local = plan_ref[2, b] - where_ref[1] * per_shard

            @pl.when((local >= 0) & (local < per_shard))
            def _():
                mine_saved_ref[rows_of(local), :] = values
                mine_grad_ref[rows_of(local), :] = grads

    upper = dot(normed[...], up_ref[...], (1, 0))
    back = (dot(upstream[...], down_ref[...], (1, 1)) * silu_slope(upper)).astype(jnp.bfloat16)
    total[...] += dot(back, up_ref[...], (1, 1))

    @pl.when(step == pl.num_programs(0) - 1)
    def _():
        sum_ref[...] = jnp.zeros_like(sum_ref)

        @pl.loop(0, blocks)
        def _(b):
            sum_ref[rows_of(plan_ref[2, b]), :] = total[rows_of(b), :].astype(jnp.bfloat16)


def run_layer(kernel, plan, where, arrays, gain, w_up, w_down, blocks, shard_rows, products):
    every, width = arrays[0].shape
    hidden = w_up.shape[1]
    tile = next(t for t in (512, 256, 128, hidden) if hidden % t == 0)
    rows = blocks * BLOCK
    whole = lambda shape: pl.BlockSpec(shape, lambda i, *_: (0, 0))
    n = len(arrays)
    return pl.pallas_call(
        functools.partial(kernel, blocks, shard_rows // BLOCK),
        grid_spec=pltpu.PrefetchScalarGridSpec(
            num_scalar_prefetch=2,
            grid=(hidden // tile,),
            in_specs=[whole((every, width))] * n
            + [
                whole((1, width)),
                pl.BlockSpec((width, tile), lambda i, *_: (0, i)),
                pl.BlockSpec((tile, width), lambda i, *_: (i, 0)),
            ],
            out_specs=[whole((every, width))] + [whole((shard_rows, width))] * n,
            scratch_shapes=[pltpu.VMEM((rows, width), jnp.bfloat16)] * n
            + [pltpu.VMEM((rows, width), jnp.float32)],
        ),
        out_shape=[jax.ShapeDtypeStruct((every, width), jnp.bfloat16)]
        + [jax.ShapeDtypeStruct((shard_rows, width), jnp.bfloat16)] * n,
        compiler_params=pltpu.CompilerParams(
            dimension_semantics=("arbitrary",), vmem_limit_bytes=VMEM_LIMIT
        ),
        cost_estimate=pl.CostEstimate(
            flops=2 * products * rows * width * hidden,
            bytes_accessed=4 * width * hidden,
            transcendentals=rows * hidden,
        ),
    )(plan, where, *arrays, gain, w_up, w_down)


def gather(own):
    return lax.all_gather(
        lax.all_gather(own, "rep", axis=0, tiled=True), "tp", axis=0, tiled=True
    )


def scatter(partial):
    near = lax.psum_scatter(partial, "tp", scatter_dimension=0, tiled=True)
    return lax.psum_scatter(near, "rep", scatter_dimension=0, tiled=True).astype(jnp.float32)


def local(
    act_forward,
    act_saved,
    grad_output,
    norm_gain,
    up_weight,
    down_weight,
    section_layers,
    redirect_count,
    redirect_dest,
):
    replicas = lax.axis_size("rep")
    shard_rows, width = act_forward.shape[2:]
    per_shard = shard_rows // BLOCK
    blocks = START * replicas
    shard = lax.axis_index("tp") * replicas + lax.axis_index("rep")
    where = jnp.stack([lax.axis_index("pipe"), shard]).astype(jnp.int32)
    plan = make_plan(where, section_layers, redirect_count, redirect_dest, replicas, per_shard)
    w_up, w_down = up_weight[0], down_weight[0]
    fresh = gather(act_forward[0, 0])
    saved = gather(act_saved[0, 0])
    upstream = gather(grad_output[0, 0])
    mixed, mine_fresh = run_layer(
        forward_kernel, plan, where, [fresh], norm_gain, w_up, w_down, blocks, shard_rows, 2
    )
    returned, mine_saved, mine_grad = run_layer(
        backward_kernel, plan, where, [saved, upstream], norm_gain, w_up, w_down, blocks, shard_rows, 3
    )
    result = (mine_fresh.astype(jnp.float32) + scatter(mixed)).astype(jnp.bfloat16)
    arrive_forward = from_behind(result, "pipe", 1)
    gradient = (
        mine_grad.astype(jnp.float32) + norm_back(mine_saved, norm_gain, scatter(returned))
    ).astype(jnp.bfloat16)
    arrive_backward = from_behind(gradient, "pipe", -1)
    return (arrive_forward[None, None], arrive_backward[None, None])


def solution(mesh):
    in_specs = (
        P("pipe", "rep", "tp", None),
        P("pipe", "rep", "tp", None),
        P("pipe", "rep", "tp", None),
        P("pipe", None),
        P("pipe", None, ("rep", "tp")),
        P("pipe", ("rep", "tp"), None),
        P(),
        P(),
        P(),
    )
    out_specs = (P("pipe", "rep", "tp", None), P("pipe", "rep", "tp", None))
    return jax.shard_map(local, mesh=mesh, in_specs=in_specs, out_specs=out_specs, check_vma=False)
```

```python
import functools

import jax
import jax.numpy as jnp
from jax import lax
from jax.experimental import pallas as pl
from jax.experimental.pallas import tpu as pltpu
from jax.sharding import PartitionSpec as P

BLOCK = 16
CAPB = 8
START = 5
EPSILON = 1e-05
VMEM_LIMIT = 52 * 1024 * 1024


def from_behind(block, axis, distance):
    devices = range(lax.axis_size(axis))
    route = [(i - distance, i) for i in devices if i - distance in devices]
    return lax.ppermute(block, axis, route)


def plan_kernel(replicas, per_shard, where_ref, layers_ref, count_ref, dest_ref, out_ref):
    bounds = layers_ref.shape[0] - 1
    position = where_ref[0]
    zero = jnp.int32(0)
    ends, seen = [], jnp.int32(-1)
    for s in range(bounds):
        seen = seen + layers_ref[s]
        ends.append(seen)
    moved = [
        [
            jnp.where((dest_ref[s, r] != r) & (count_ref[s, r] > 0), count_ref[s, r], 0)
            for r in range(replicas)
        ]
        for s in range(bounds)
    ]

    def place(replica, block):
        return (lax.div(block, per_shard) * replicas + replica) * per_shard + lax.rem(block, per_shard)

    for which in range(2):
        at = position if which == 0 else jnp.maximum(position - 1, 0)
        live = [jnp.int32(START) for _ in range(replicas)]
        mine = [zero for _ in range(replicas)]
        to = [jnp.int32(r) for r in range(replicas)]
        for s in range(bounds):
            before, here = ends[s] < at, ends[s] == at
            for q in range(replicas):
                gain = -moved[s][q]
                for r in range(replicas):
                    gain = gain + jnp.where(dest_ref[s, r] == q, moved[s][r], 0)
                live[q] = live[q] + jnp.where(before, gain, 0)
                mine[q] = jnp.where(here, moved[s][q], mine[q])
                to[q] = jnp.where(here, dest_ref[s, q], to[q])
        incoming = [
            sum((jnp.where(to[r] == q, mine[r], 0) for r in range(replicas)), zero)
            for q in range(replicas)
        ]
        offset = [
            sum((jnp.where(to[o] == to[r], mine[o], 0) for o in range(r)), zero)
            for r in range(replicas)
        ]
        filled = zero
        for q in range(replicas):
            for k in range(CAPB):
                local = k - incoming[q]
                own = (local >= 0) & (local < live[q] - mine[q])
                source = jnp.where(own, place(jnp.int32(q), jnp.maximum(local + mine[q], 0)), -1)
                for r in range(replicas):
                    hit = (mine[r] > 0) & (to[r] == q) & (k >= offset[r]) & (k < offset[r] + mine[r])
                    source = jnp.where(
                        hit, place(jnp.int32(r), jnp.maximum(k - offset[r], 0)), source
                    )
                target = place(jnp.int32(q), jnp.int32(k))
                out_ref[2 * which, filled] = jnp.maximum(source, 0)
                out_ref[2 * which + 1, filled] = target
                filled = filled + jnp.where(source >= 0, 1, 0)


def make_plan(where, section_layers, redirect_count, redirect_dest, replicas, per_shard):
    return pl.pallas_call(
        functools.partial(plan_kernel, replicas, per_shard),
        out_shape=jax.ShapeDtypeStruct((4, replicas * CAPB + 1), jnp.int32),
        in_specs=[pl.BlockSpec(memory_space=pltpu.SMEM)] * 4,
        out_specs=pl.BlockSpec(memory_space=pltpu.SMEM),
    )(where, section_layers, redirect_count, redirect_dest)


def normalize(values, gain_row):
    wide = values.astype(jnp.float32)
    scale = lax.rsqrt(jnp.mean(wide * wide, axis=-1, keepdims=True) + EPSILON)
    return (wide * scale * gain_row.astype(jnp.float32)).astype(jnp.bfloat16)


def norm_back(values, gain_row, upstream):
    wide = values.astype(jnp.float32)
    scale = lax.rsqrt(jnp.mean(wide * wide, axis=-1, keepdims=True) + EPSILON)
    weighted = gain_row.astype(jnp.float32) * upstream
    return scale * weighted - wide * (scale * scale * scale) * jnp.mean(
        weighted * wide, axis=-1, keepdims=True
    )


def silu_slope(upper):
    sigma = jax.nn.sigmoid(upper)
    return sigma * (1.0 + upper * (1.0 - sigma))


def dot(left, right, contract):
    return lax.dot_general(
        left, right, ((contract[:1], contract[1:]), ((), ())), preferred_element_type=jnp.float32
    )


def for_source(block, per_shard, shard, arrays, body):
    if len(arrays[0]) == 1:
        body(*(pieces[0][rows_of(block), :] for pieces in arrays))
        return
    piece = lax.bitwise_xor(lax.div(block, per_shard), shard)
    inside = rows_of(lax.rem(block, per_shard))
    for i in range(len(arrays[0])):

        @pl.when(piece == i)
        def _():
            body(*(pieces[i][inside, :] for pieces in arrays))


def rows_of(block):
    return pl.ds(pl.multiple_of(block * BLOCK, BLOCK), BLOCK)


def forward_kernel(
    blocks, per_shard, parts, plan_ref, where_ref, *refs
):
    fresh, refs = refs[:parts], refs[parts:]
    gain_ref, up_ref, down_ref, sum_ref, mine_ref, normed, total = refs
    step = pl.program_id(0)

    @pl.when(step == 0)
    def _():
        total[...] = jnp.zeros_like(total)
        mine_ref[...] = jnp.zeros_like(mine_ref)

        @pl.loop(0, blocks)
        def _(b):
            local = plan_ref[1, b] - where_ref[1] * per_shard

            def place(values):
                normed[rows_of(b), :] = normalize(values, gain_ref[...])

                @pl.when((local >= 0) & (local < per_shard))
                def _():
                    mine_ref[rows_of(local), :] = values

            for_source(plan_ref[0, b], per_shard, where_ref[1], [fresh], place)

    hidden = jax.nn.silu(dot(normed[...], up_ref[...], (1, 0))).astype(jnp.bfloat16)
    total[...] += dot(hidden, down_ref[...], (1, 0))

    @pl.when(step == pl.num_programs(0) - 1)
    def _():
        sum_ref[...] = jnp.zeros_like(sum_ref)

        @pl.loop(0, blocks)
        def _(b):
            sum_ref[rows_of(plan_ref[1, b]), :] = total[rows_of(b), :].astype(jnp.bfloat16)


def backward_kernel(
    blocks, per_shard, parts, plan_ref, where_ref, *refs
):
    saved, grad, refs = refs[:parts], refs[parts : 2 * parts], refs[2 * parts :]
    gain_ref, up_ref, down_ref, sum_ref, mine_saved_ref, mine_grad_ref = refs[:6]
    normed, upstream, total = refs[6:]
    step = pl.program_id(0)

    @pl.when(step == 0)
    def _():
        total[...] = jnp.zeros_like(total)
        mine_saved_ref[...] = jnp.zeros_like(mine_saved_ref)
        mine_grad_ref[...] = jnp.zeros_like(mine_grad_ref)

        @pl.loop(0, blocks)
        def _(b):
            local = plan_ref[2, b] - where_ref[1] * per_shard

            def place(values, grads):
                normed[rows_of(b), :] = normalize(values, gain_ref[...])
                upstream[rows_of(b), :] = grads

                @pl.when((local >= 0) & (local < per_shard))
                def _():
                    mine_saved_ref[rows_of(local), :] = values
                    mine_grad_ref[rows_of(local), :] = grads

            for_source(plan_ref[3, b], per_shard, where_ref[1], [saved, grad], place)

    upper = dot(normed[...], up_ref[...], (1, 0))
    back = (dot(upstream[...], down_ref[...], (1, 1)) * silu_slope(upper)).astype(jnp.bfloat16)
    total[...] += dot(back, up_ref[...], (1, 1))

    @pl.when(step == pl.num_programs(0) - 1)
    def _():
        sum_ref[...] = jnp.zeros_like(sum_ref)

        @pl.loop(0, blocks)
        def _(b):
            sum_ref[rows_of(plan_ref[2, b]), :] = total[rows_of(b), :].astype(jnp.bfloat16)


def run_layer(kernel, plan, where, arrays, gain, w_up, w_down, blocks, shard_rows, products):
    parts = len(arrays[0])
    piece_rows, width = arrays[0][0].shape
    every = parts * piece_rows
    hidden = w_up.shape[1]
    tile = next(t for t in (512, 256, 128, hidden) if hidden % t == 0)
    rows = blocks * BLOCK
    whole = lambda shape: pl.BlockSpec(shape, lambda i, *_: (0, 0))
    n = len(arrays)
    return pl.pallas_call(
        functools.partial(kernel, blocks, shard_rows // BLOCK, parts),
        grid_spec=pltpu.PrefetchScalarGridSpec(
            num_scalar_prefetch=2,
            grid=(hidden // tile,),
            in_specs=[whole((piece_rows, width))] * (n * parts)
            + [
                whole((1, width)),
                pl.BlockSpec((width, tile), lambda i, *_: (0, i)),
                pl.BlockSpec((tile, width), lambda i, *_: (i, 0)),
            ],
            out_specs=[whole((every, width))] + [whole((shard_rows, width))] * n,
            scratch_shapes=[pltpu.VMEM((rows, width), jnp.bfloat16)] * n
            + [pltpu.VMEM((rows, width), jnp.float32)],
        ),
        out_shape=[jax.ShapeDtypeStruct((every, width), jnp.bfloat16)]
        + [jax.ShapeDtypeStruct((shard_rows, width), jnp.bfloat16)] * n,
        compiler_params=pltpu.CompilerParams(
            dimension_semantics=("arbitrary",), vmem_limit_bytes=VMEM_LIMIT
        ),
        cost_estimate=pl.CostEstimate(
            flops=2 * products * rows * width * hidden,
            bytes_accessed=4 * width * hidden,
            transcendentals=rows * hidden,
        ),
    )(plan, where, *(piece for pieces in arrays for piece in pieces), gain, w_up, w_down)


def other(block, axis):
    return lax.ppermute(block, axis, [(0, 1), (1, 0)])


def in_pairs():
    return lax.axis_size("rep") == 2 and lax.axis_size("tp") == 2


def gather(own, across=None):
    if in_pairs():
        across = other(own, "rep") if across is None else across
        return [own, across, other(own, "tp"), other(across, "tp")]
    return [
        lax.all_gather(lax.all_gather(own, "rep", axis=0, tiled=True), "tp", axis=0, tiled=True)
    ]


def half(block, index):
    rows = block.shape[0] // 2
    return lax.dynamic_slice_in_dim(block, index * rows, rows)


def scatter(partial):
    if in_pairs():
        for axis in ("tp", "rep"):
            index = lax.axis_index(axis)
            arrived = other(half(partial, 1 - index), axis)
            partial = half(partial, index).astype(jnp.float32) + arrived.astype(jnp.float32)
            if axis == "tp":
                partial = partial.astype(jnp.bfloat16)
        return partial
    near = lax.psum_scatter(partial, "tp", scatter_dimension=0, tiled=True)
    return lax.psum_scatter(near, "rep", scatter_dimension=0, tiled=True).astype(jnp.float32)


def scatter_direct(partial, shard, shard_rows):
    if not in_pairs():
        return scatter(partial), []
    piece = lambda k: lax.dynamic_slice_in_dim(partial, lax.bitwise_xor(shard, k) * shard_rows, shard_rows)
    arrived = [
        other(piece(1), "rep"),
        lax.ppermute(piece(3), ("rep", "tp"), [(i, 3 - i) for i in range(4)]),
        other(piece(2), "tp"),
    ]
    return piece(0).astype(jnp.float32), arrived


def local(
    act_forward,
    act_saved,
    grad_output,
    norm_gain,
    up_weight,
    down_weight,
    section_layers,
    redirect_count,
    redirect_dest,
):
    replicas = lax.axis_size("rep")
    shard_rows, width = act_forward.shape[2:]
    per_shard = shard_rows // BLOCK
    blocks = START * replicas
    shard = lax.axis_index("tp") * replicas + lax.axis_index("rep")
    where = jnp.stack([lax.axis_index("pipe"), shard]).astype(jnp.int32)
    plan = make_plan(where, section_layers, redirect_count, redirect_dest, replicas, per_shard)
    w_up, w_down = up_weight[0], down_weight[0]
    fresh_own, saved_own, grad_own = act_forward[0, 0], act_saved[0, 0], grad_output[0, 0]
    fresh_across = None
    if in_pairs():
        fresh_across, saved_own, grad_own = lax.optimization_barrier(
            (other(fresh_own, "rep"), saved_own, grad_own)
        )
    fresh = gather(fresh_own, fresh_across)
    saved, upstream = gather(saved_own), gather(grad_own)
    mixed, mine_fresh = run_layer(
        forward_kernel, plan, where, [fresh], norm_gain, w_up, w_down, blocks, shard_rows, 2
    )
    mixed, plan = lax.optimization_barrier((mixed, plan))
    total, arrived = scatter_direct(mixed, shard, shard_rows)
    returned, mine_saved, mine_grad = run_layer(
        backward_kernel, plan, where, [saved, upstream], norm_gain, w_up, w_down, blocks, shard_rows, 3
    )
    for block in arrived:
        total = total + block.astype(jnp.float32)
    result = (mine_fresh.astype(jnp.float32) + total).astype(jnp.bfloat16)
    arrive_forward = from_behind(result, "pipe", 1)
    gradient = (
        mine_grad.astype(jnp.float32) + norm_back(mine_saved, norm_gain, scatter(returned))
    ).astype(jnp.bfloat16)
    arrive_backward = from_behind(gradient, "pipe", -1)
    return (arrive_forward[None, None], arrive_backward[None, None])


def solution(mesh):
    in_specs = (
        P("pipe", "rep", "tp", None),
        P("pipe", "rep", "tp", None),
        P("pipe", "rep", "tp", None),
        P("pipe", None),
        P("pipe", None, ("rep", "tp")),
        P("pipe", ("rep", "tp"), None),
        P(),
        P(),
        P(),
    )
    out_specs = (P("pipe", "rep", "tp", None), P("pipe", "rep", "tp", None))
    return jax.shard_map(local, mesh=mesh, in_specs=in_specs, out_specs=out_specs, check_vma=False)
```

```python
import functools

import jax
import jax.numpy as jnp
from jax import lax
from jax.experimental import pallas as pl
from jax.experimental.pallas import tpu as pltpu
from jax.sharding import PartitionSpec as P

BLOCK = 16
CAPB = 8
START = 5
EPSILON = 1e-05
VMEM_LIMIT = 52 * 1024 * 1024


def from_behind(block, axis, distance):
    devices = range(lax.axis_size(axis))
    route = [(i - distance, i) for i in devices if i - distance in devices]
    return lax.ppermute(block, axis, route)


def plan_kernel(replicas, per_shard, where_ref, layers_ref, count_ref, dest_ref, out_ref):
    bounds = layers_ref.shape[0] - 1
    position = where_ref[0]
    zero = jnp.int32(0)
    ends, seen = [], jnp.int32(-1)
    for s in range(bounds):
        seen = seen + layers_ref[s]
        ends.append(seen)
    moved = [
        [
            jnp.where((dest_ref[s, r] != r) & (count_ref[s, r] > 0), count_ref[s, r], 0)
            for r in range(replicas)
        ]
        for s in range(bounds)
    ]

    def place(replica, block):
        return (lax.div(block, per_shard) * replicas + replica) * per_shard + lax.rem(block, per_shard)

    for which in range(2):
        at = position if which == 0 else jnp.maximum(position - 1, 0)
        live = [jnp.int32(START) for _ in range(replicas)]
        mine = [zero for _ in range(replicas)]
        to = [jnp.int32(r) for r in range(replicas)]
        for s in range(bounds):
            before, here = ends[s] < at, ends[s] == at
            for q in range(replicas):
                gain = -moved[s][q]
                for r in range(replicas):
                    gain = gain + jnp.where(dest_ref[s, r] == q, moved[s][r], 0)
                live[q] = live[q] + jnp.where(before, gain, 0)
                mine[q] = jnp.where(here, moved[s][q], mine[q])
                to[q] = jnp.where(here, dest_ref[s, q], to[q])
        incoming = [
            sum((jnp.where(to[r] == q, mine[r], 0) for r in range(replicas)), zero)
            for q in range(replicas)
        ]
        offset = [
            sum((jnp.where(to[o] == to[r], mine[o], 0) for o in range(r)), zero)
            for r in range(replicas)
        ]
        filled = zero
        for q in range(replicas):
            for k in range(CAPB):
                local = k - incoming[q]
                own = (local >= 0) & (local < live[q] - mine[q])
                source = jnp.where(own, place(jnp.int32(q), jnp.maximum(local + mine[q], 0)), -1)
                for r in range(replicas):
                    hit = (mine[r] > 0) & (to[r] == q) & (k >= offset[r]) & (k < offset[r] + mine[r])
                    source = jnp.where(
                        hit, place(jnp.int32(r), jnp.maximum(k - offset[r], 0)), source
                    )
                target = place(jnp.int32(q), jnp.int32(k))
                out_ref[2 * which, filled] = jnp.maximum(source, 0)
                out_ref[2 * which + 1, filled] = target
                filled = filled + jnp.where(source >= 0, 1, 0)


def make_plan(where, section_layers, redirect_count, redirect_dest, replicas, per_shard):
    return pl.pallas_call(
        functools.partial(plan_kernel, replicas, per_shard),
        out_shape=jax.ShapeDtypeStruct((4, replicas * CAPB + 1), jnp.int32),
        in_specs=[pl.BlockSpec(memory_space=pltpu.SMEM)] * 4,
        out_specs=pl.BlockSpec(memory_space=pltpu.SMEM),
    )(where, section_layers, redirect_count, redirect_dest)


def normalize(values, gain_row):
    wide = values.astype(jnp.float32)
    scale = lax.rsqrt(jnp.mean(wide * wide, axis=-1, keepdims=True) + EPSILON)
    return (wide * scale * gain_row.astype(jnp.float32)).astype(jnp.bfloat16)


def norm_back(values, gain_row, upstream):
    wide = values.astype(jnp.float32)
    scale = lax.rsqrt(jnp.mean(wide * wide, axis=-1, keepdims=True) + EPSILON)
    weighted = gain_row.astype(jnp.float32) * upstream
    return scale * weighted - wide * (scale * scale * scale) * jnp.mean(
        weighted * wide, axis=-1, keepdims=True
    )


def silu_slope(upper):
    sigma = jax.nn.sigmoid(upper)
    return sigma * (1.0 + upper * (1.0 - sigma))


def dot(left, right, contract):
    return lax.dot_general(
        left, right, ((contract[:1], contract[1:]), ((), ())), preferred_element_type=jnp.float32
    )


def for_source(block, per_shard, shard, arrays, body):
    if len(arrays[0]) == 1:
        body(*(pieces[0][rows_of(block), :] for pieces in arrays))
        return
    piece = lax.bitwise_xor(lax.div(block, per_shard), shard)
    inside = rows_of(lax.rem(block, per_shard))
    for i in range(len(arrays[0])):

        @pl.when(piece == i)
        def _():
            body(*(pieces[i][inside, :] for pieces in arrays))


def rows_of(block):
    return pl.ds(pl.multiple_of(block * BLOCK, BLOCK), BLOCK)


def forward_kernel(
    blocks, per_shard, parts, plan_ref, where_ref, *refs
):
    fresh, refs = refs[:parts], refs[parts:]
    gain_ref, up_ref, down_ref, sum_ref, mine_ref, normed, total = refs
    step = pl.program_id(0)

    @pl.when(step == 0)
    def _():
        total[...] = jnp.zeros_like(total)
        mine_ref[...] = jnp.zeros_like(mine_ref)

        @pl.loop(0, blocks)
        def _(b):
            local = plan_ref[1, b] - where_ref[1] * per_shard

            def place(values):
                normed[rows_of(b), :] = normalize(values, gain_ref[...])

                @pl.when((local >= 0) & (local < per_shard))
                def _():
                    mine_ref[rows_of(local), :] = values

            for_source(plan_ref[0, b], per_shard, where_ref[1], [fresh], place)

    hidden = jax.nn.silu(dot(normed[...], up_ref[...], (1, 0))).astype(jnp.bfloat16)
    total[...] += dot(hidden, down_ref[...], (1, 0))

    @pl.when(step == pl.num_programs(0) - 1)
    def _():
        sum_ref[...] = jnp.zeros_like(sum_ref)

        @pl.loop(0, blocks)
        def _(b):
            sum_ref[rows_of(plan_ref[1, b]), :] = total[rows_of(b), :].astype(jnp.bfloat16)


def backward_kernel(
    blocks, per_shard, parts, plan_ref, where_ref, *refs
):
    saved, grad, refs = refs[:parts], refs[parts : 2 * parts], refs[2 * parts :]
    gain_ref, up_ref, down_ref, sum_ref, mine_saved_ref, mine_grad_ref = refs[:6]
    normed, upstream, total = refs[6:]
    step = pl.program_id(0)

    @pl.when(step == 0)
    def _():
        total[...] = jnp.zeros_like(total)
        mine_saved_ref[...] = jnp.zeros_like(mine_saved_ref)
        mine_grad_ref[...] = jnp.zeros_like(mine_grad_ref)

        @pl.loop(0, blocks)
        def _(b):
            local = plan_ref[2, b] - where_ref[1] * per_shard

            def place(values, grads):
                normed[rows_of(b), :] = normalize(values, gain_ref[...])
                upstream[rows_of(b), :] = grads

                @pl.when((local >= 0) & (local < per_shard))
                def _():
                    mine_saved_ref[rows_of(local), :] = values
                    mine_grad_ref[rows_of(local), :] = grads

            for_source(plan_ref[3, b], per_shard, where_ref[1], [saved, grad], place)

    upper = dot(normed[...], up_ref[...], (1, 0))
    back = (dot(upstream[...], down_ref[...], (1, 1)) * silu_slope(upper)).astype(jnp.bfloat16)
    total[...] += dot(back, up_ref[...], (1, 1))

    @pl.when(step == pl.num_programs(0) - 1)
    def _():
        sum_ref[...] = jnp.zeros_like(sum_ref)

        @pl.loop(0, blocks)
        def _(b):
            sum_ref[rows_of(plan_ref[2, b]), :] = total[rows_of(b), :].astype(jnp.bfloat16)


def run_layer(kernel, plan, where, arrays, gain, w_up, w_down, blocks, shard_rows, products):
    parts = len(arrays[0])
    piece_rows, width = arrays[0][0].shape
    every = parts * piece_rows
    hidden = w_up.shape[1]
    tile = next(t for t in (512, 256, 128, hidden) if hidden % t == 0)
    rows = blocks * BLOCK
    whole = lambda shape: pl.BlockSpec(shape, lambda i, *_: (0, 0))
    n = len(arrays)
    return pl.pallas_call(
        functools.partial(kernel, blocks, shard_rows // BLOCK, parts),
        grid_spec=pltpu.PrefetchScalarGridSpec(
            num_scalar_prefetch=2,
            grid=(hidden // tile,),
            in_specs=[whole((piece_rows, width))] * (n * parts)
            + [
                whole((1, width)),
                pl.BlockSpec((width, tile), lambda i, *_: (0, i)),
                pl.BlockSpec((tile, width), lambda i, *_: (i, 0)),
            ],
            out_specs=[whole((every, width))] + [whole((shard_rows, width))] * n,
            scratch_shapes=[pltpu.VMEM((rows, width), jnp.bfloat16)] * n
            + [pltpu.VMEM((rows, width), jnp.float32)],
        ),
        out_shape=[jax.ShapeDtypeStruct((every, width), jnp.bfloat16)]
        + [jax.ShapeDtypeStruct((shard_rows, width), jnp.bfloat16)] * n,
        compiler_params=pltpu.CompilerParams(
            dimension_semantics=("arbitrary",), vmem_limit_bytes=VMEM_LIMIT
        ),
        cost_estimate=pl.CostEstimate(
            flops=2 * products * rows * width * hidden,
            bytes_accessed=4 * width * hidden,
            transcendentals=rows * hidden,
        ),
    )(plan, where, *(piece for pieces in arrays for piece in pieces), gain, w_up, w_down)


def other(block, axis):
    return lax.ppermute(block, axis, [(0, 1), (1, 0)])


def in_pairs():
    return lax.axis_size("rep") == 2 and lax.axis_size("tp") == 2


def gather(own, across=None):
    if in_pairs():
        across = other(own, "rep") if across is None else across
        return [own, across, other(own, "tp"), other(across, "tp")]
    return [
        lax.all_gather(lax.all_gather(own, "rep", axis=0, tiled=True), "tp", axis=0, tiled=True)
    ]


def half(block, index):
    rows = block.shape[0] // 2
    return lax.dynamic_slice_in_dim(block, index * rows, rows)


def scatter_near(partial):
    if in_pairs():
        index = lax.axis_index("tp")
        arrived = other(half(partial, 1 - index), "tp")
        near = half(partial, index).astype(jnp.float32) + arrived.astype(jnp.float32)
        return near.astype(jnp.bfloat16)
    return lax.psum_scatter(partial, "tp", scatter_dimension=0, tiled=True)


def scatter_far(near):
    if in_pairs():
        index = lax.axis_index("rep")
        arrived = other(half(near, 1 - index), "rep")
        return half(near, index).astype(jnp.float32) + arrived.astype(jnp.float32)
    return lax.psum_scatter(near, "rep", scatter_dimension=0, tiled=True).astype(jnp.float32)


def local(
    act_forward,
    act_saved,
    grad_output,
    norm_gain,
    up_weight,
    down_weight,
    section_layers,
    redirect_count,
    redirect_dest,
):
    replicas = lax.axis_size("rep")
    shard_rows, width = act_forward.shape[2:]
    per_shard = shard_rows // BLOCK
    blocks = START * replicas
    shard = lax.axis_index("tp") * replicas + lax.axis_index("rep")
    where = jnp.stack([lax.axis_index("pipe"), shard]).astype(jnp.int32)
    plan = make_plan(where, section_layers, redirect_count, redirect_dest, replicas, per_shard)
    w_up, w_down = up_weight[0], down_weight[0]
    fresh_own, saved_own, grad_own = act_forward[0, 0], act_saved[0, 0], grad_output[0, 0]
    fresh_across = None
    if in_pairs():
        fresh_across, saved_own, grad_own = lax.optimization_barrier(
            (other(fresh_own, "rep"), saved_own, grad_own)
        )
    fresh = gather(fresh_own, fresh_across)
    saved_across = grad_across = None
    if in_pairs():
        saved_across, grad_across = other(saved_own, "rep"), other(grad_own, "rep")
    mixed, mine_fresh = run_layer(
        forward_kernel, plan, where, [fresh], norm_gain, w_up, w_down, blocks, shard_rows, 2
    )
    if in_pairs():
        mixed, saved_across, grad_across = lax.optimization_barrier(
            (mixed, saved_across, grad_across)
        )
    saved, upstream = gather(saved_own, saved_across), gather(grad_own, grad_across)
    near, plan = lax.optimization_barrier((scatter_near(mixed), plan))
    returned, mine_saved, mine_grad = run_layer(
        backward_kernel, plan, where, [saved, upstream], norm_gain, w_up, w_down, blocks, shard_rows, 3
    )
    result = (mine_fresh.astype(jnp.float32) + scatter_far(near)).astype(jnp.bfloat16)
    arrive_forward = from_behind(result, "pipe", 1)
    gradient = (
        mine_grad.astype(jnp.float32) + norm_back(mine_saved, norm_gain, scatter_far(scatter_near(returned)))
    ).astype(jnp.bfloat16)
    arrive_backward = from_behind(gradient, "pipe", -1)
    return (arrive_forward[None, None], arrive_backward[None, None])


def solution(mesh):
    in_specs = (
        P("pipe", "rep", "tp", None),
        P("pipe", "rep", "tp", None),
        P("pipe", "rep", "tp", None),
        P("pipe", None),
        P("pipe", None, ("rep", "tp")),
        P("pipe", ("rep", "tp"), None),
        P(),
        P(),
        P(),
    )
    out_specs = (P("pipe", "rep", "tp", None), P("pipe", "rep", "tp", None))
    return jax.shard_map(local, mesh=mesh, in_specs=in_specs, out_specs=out_specs, check_vma=False)
```
